1024 devices in a mesh: horiz: 128 (over y, z), lev: 8 (over x, core).
Axes of the slice: x: 4, y: 4, z: 32, core: 2. Of those that a mesh axis runs over, the one named last changes fastest.
Arguments:
- atm_state: float32 [4, 16, 16, 32768], P(None, 'lev', None, 'horiz'), may hold values from -6 to 6
- atm_mixing: float32 [4, 16], P(None, 'lev'), may hold values from 0.05 to 0.45
- element_operator: float32 [16, 16], replicated, may hold values from -1.5 to 1.5
- ocean_state: float32 [2, 16, 524288], P(None, 'lev', 'horiz'), may hold values from -6 to 6
- ocean_mixing: float32 [2, 16], P(None, 'lev'), may hold values from 0.05 to 0.45
- atm_flux: bfloat16 [16, 32768], P(None, 'horiz'), may hold values from -6 to 6
- sea_temp: bfloat16 [524288], P('horiz'), may hold values from -6 to 6
- ocean_tiles: bfloat16 [10240, 128, 128], P(('horiz', 'lev')), may hold values from -0.5 to 0.5
- ocean_tile_src: int32 [10240], P(('horiz', 'lev')), may hold values from 0 to 31
- ocean_tile_dst: int32 [10240], P(('horiz', 'lev')), may hold values from 0 to 32, as said below
- atmos_tiles: bfloat16 [10240, 128, 128], P(('horiz', 'lev')), may hold values from -0.5 to 0.5
- atmos_tile_src: int32 [10240], P(('horiz', 'lev')), may hold values from 0 to 31
- atmos_tile_dst: int32 [10240], P(('horiz', 'lev')), may hold values from 0 to 32, as said below
Outputs:
- atm_next: float32 [4, 16, 16, 32768], P(None, 'lev', None, 'horiz')
- ocean_next: float32 [2, 16, 524288], P(None, 'lev', 'horiz')
The draws below stay inside these ranges and needn't reach their ends.
Inputs may be any that keep to these rules, and one draw needn't show every extreme that they name: `ocean_tile_dst`: entry i of a receiver h, l describes the inbound slot from sender (h - (o - 2)) mod 128, l, reach o, place c; it names a local ocean block, or 32 for an empty slot; every local ocean block is named by at least one entry of each receiver h. `atmos_tile_dst`: entry i of a receiver h, l describes the inbound slot from sender (h - (o - 2)) mod 128, l, reach o, place c; it names a local atmosphere block, or 32 for an empty slot; every local atmosphere block is named by at least one entry of each receiver h.
All inputs are finite; a program needn't handle non-finite values.
Results may differ from the reference program's by a relative error of at most 0.00045.
Values may be sent and summed in bfloat16 or wider, within the bound.
No kernel may reach another device: no remote copies, remote signals or barrier semaphores. Data moves between devices by JAX's collectives and lax.ppermute only.
A program may use at most 32 MiB of HBM per device.

```python
import math
import jax
import jax.numpy as jnp
from jax import lax

ELEM_DEV = 256
OCELL_DEV = 4096
NODES = 16
BLOCK = 128
NEAR = 2
CAP = 2
LEVELS = 16
OCN_LEVELS = 16
ATM_ELEMS = 32768
OCN_CELLS = 524288
SLOTS = 10
TILES = 10240
N_HORIZ = 128
N_LEV = 8


def inbound_table(key, blocks):
    first, second, third, fourth = jax.random.split(key, 4)
    width = N_LEV * SLOTS
    live_level = jax.random.randint(first, (N_HORIZ, 1), 0, 4)
    chance = jax.random.randint(second, (N_HORIZ, width), 0, 4)
    target = jax.random.randint(third, (N_HORIZ, width), 0, blocks)
    rank = jnp.arange(width, dtype=jnp.int32)[None, :]
    extra = jnp.where(chance <= live_level, target, blocks)
    values = jnp.where(rank < blocks, rank, extra)
    values = jnp.where(rank == width - 1, blocks, values).astype(jnp.int32)
    row_keys = jax.random.split(fourth, N_HORIZ)
    orders = jax.vmap(lambda k: jax.random.permutation(k, width))(row_keys)
    placed = jax.vmap(lambda where, what: jnp.zeros((width,), jnp.int32).at[where].set(what))(orders, values)
    return placed.reshape(-1).astype(jnp.int32)


def draw_ocean_tile_dst(key, part):
    key = jax.random.fold_in(key, 11)
    return inbound_table(key, OCELL_DEV // BLOCK)


def draw_atmos_tile_dst(key, part):
    key = jax.random.fold_in(key, 12)
    return inbound_table(key, NODES * ELEM_DEV // BLOCK)


def touch_ends(array, key, low, top_value):
    place = [jax.random.randint(jax.random.fold_in(key, axis), (), 0, length) for axis, length in enumerate(array.shape)]
    widest = array.shape.index(max(array.shape))
    next_to = place[:widest] + [(place[widest] + 1) % array.shape[widest]] + place[widest + 1:]
    return array.at[tuple(place)].set(low).at[tuple(next_to)].set(top_value)


def block_scale(stream_key, shape, shards, least, top_value):
    level = 1.0
    for axis_at, shards_of in shards:
        heights = jax.random.uniform(jax.random.fold_in(jax.random.fold_in(stream_key, 6), axis_at), (shards_of,), jnp.float32, least / len(shards), top_value / len(shards))
        level = level * jnp.repeat(jnp.exp(heights), shape[axis_at] // shards_of).reshape((-1,) + (1,) * (len(shape) - 1 - axis_at))
    return level


def normal_values(rng, extent, scale, most, cuts=(), kind=jnp.bfloat16):
    values = jax.random.normal(rng, extent, jnp.float32) * scale
    if len(cuts) > 0:
        values = block_scale(rng, extent, cuts, -0.22, 0.18) * values
    return jnp.clip(values, min=-most, max=most).astype(kind)


def setup_inputs(seed: int = 0) -> dict:
    key_of = jax.random.split(jax.random.key(seed), 14)
    atm_state = normal_values(key_of[0], (4, LEVELS, NODES, ATM_ELEMS), 1.0, 6.0, ((1, 8), (3, 128)), jnp.float32)
    atm_mixing = jnp.clip(jnp.exp(math.log(0.45) - 2.1972245 * jax.random.uniform(key_of[1], (4, LEVELS), jnp.float32) ** block_scale(key_of[1], (4, LEVELS), ((1, 8),), -0.2, 0.2)), 0.05, 0.45)
    element_operator = normal_values(key_of[2], (NODES, NODES), NODES ** -0.5, 1.5, (), jnp.float32)
    ocean_state = normal_values(key_of[3], (2, OCN_LEVELS, OCN_CELLS), 1.0, 6.0, ((1, 8), (2, 128)), jnp.float32)
    ocean_mixing = jnp.clip(jnp.exp(math.log(0.45) - 2.1972245 * jax.random.uniform(key_of[4], (2, OCN_LEVELS), jnp.float32) ** block_scale(key_of[4], (2, OCN_LEVELS), ((1, 8),), -0.2, 0.2)), 0.05, 0.45)
    atm_flux = normal_values(key_of[5], (NODES, ATM_ELEMS), 1.0, 6.0, ((1, 128),))
    sea_temp = normal_values(key_of[6], (OCN_CELLS,), 1.0, 6.0, ((0, 128),))
    ocean_tiles = normal_values(key_of[7], (TILES, BLOCK, BLOCK), BLOCK ** -0.5, 0.5, ((0, 1024),))
    ocean_tile_src = touch_ends(jax.random.randint(key_of[8], (TILES,), 0, NODES * ELEM_DEV // BLOCK), jax.random.fold_in(key_of[8], 1), 0, (NODES * ELEM_DEV // BLOCK) - 1).astype(jnp.int32)
    ocean_tile_dst = draw_ocean_tile_dst(jax.random.fold_in(key_of[13], 71), 0)
    atmos_tiles = normal_values(key_of[10], (TILES, BLOCK, BLOCK), BLOCK ** -0.5, 0.5, ((0, 1024),))
    atmos_tile_src = touch_ends(jax.random.randint(key_of[11], (TILES,), 0, OCELL_DEV // BLOCK), jax.random.fold_in(key_of[11], 1), 0, (OCELL_DEV // BLOCK) - 1).astype(jnp.int32)
    atmos_tile_dst = draw_atmos_tile_dst(jax.random.fold_in(key_of[13], 71), 0)
    return {"atm_state": atm_state, "atm_mixing": atm_mixing, "element_operator": element_operator, "ocean_state": ocean_state, "ocean_mixing": ocean_mixing, "atm_flux": atm_flux, "sea_temp": sea_temp, "ocean_tiles": ocean_tiles, "ocean_tile_src": ocean_tile_src, "ocean_tile_dst": ocean_tile_dst, "atmos_tiles": atmos_tiles, "atmos_tile_src": atmos_tile_src, "atmos_tile_dst": atmos_tile_dst}


def vertical(fields, mixing):
    beneath = jnp.concatenate([fields[:, :1], fields[:, :-1]], axis=1)
    overhead = jnp.concatenate([fields[:, 1:], fields[:, -1:]], axis=1)
    mix_rate = mixing.reshape(mixing.shape + (1,) * (fields.ndim - 2))
    return fields + mix_rate * (overhead - 2.0 * fields + beneath)


def remap(tile_mats, src_ids, dest_ids, field_blocks, out_blocks):
    reach = 2 * NEAR + 1
    mats = tile_mats.reshape(N_HORIZ, N_LEV, reach, CAP, BLOCK, BLOCK)
    sources = src_ids.reshape(N_HORIZ, N_LEV, reach, CAP)

    def one_device(bundle):
        weights, picks, blocks = bundle
        picked = blocks[picks]
        return jnp.einsum('lzcij,lzcj->lzci', weights.astype(jnp.float32), picked.astype(jnp.float32),
                          precision=lax.Precision.HIGHEST).astype(jnp.bfloat16)

    payload = lax.map(one_device, (mats, sources, field_blocks))
    inbound = jnp.stack([jnp.roll(payload[:, :, offset_idx], offset_idx - NEAR, axis=0)
                         for offset_idx in range(reach)], axis=2)
    targets = dest_ids.reshape(N_HORIZ, N_LEV * reach * CAP)
    onehot = (targets[:, :, None] == jnp.arange(out_blocks, dtype=jnp.int32)[None, None, :]).astype(jnp.float32)
    flat_in = inbound.reshape(N_HORIZ, N_LEV * reach * CAP, BLOCK).astype(jnp.float32)
    return jnp.einsum('psb,psk->pbk', onehot, flat_in, precision=lax.Precision.HIGHEST)


def reference(atm_state, atm_mixing, element_operator, ocean_state, ocean_mixing, atm_flux, sea_temp,
              ocean_tiles, ocean_tile_src, ocean_tile_dst, atmos_tiles, atmos_tile_src, atmos_tile_dst):
    atm_blocks = atm_flux.reshape(NODES, N_HORIZ, ELEM_DEV).transpose(1, 0, 2).reshape(N_HORIZ, -1, BLOCK)
    sea_blocks = sea_temp.reshape(N_HORIZ, -1, BLOCK)
    heat_in = remap(ocean_tiles, ocean_tile_src, ocean_tile_dst, atm_blocks, OCELL_DEV // BLOCK).reshape(-1)
    temp_in = remap(atmos_tiles, atmos_tile_src, atmos_tile_dst, sea_blocks, NODES * ELEM_DEV // BLOCK)
    temp_in = temp_in.reshape(N_HORIZ, NODES, ELEM_DEV).transpose(1, 0, 2).reshape(NODES, -1)
    mixed = vertical(atm_state, atm_mixing)
    lateral = jnp.einsum('ij,fkje->fkie', element_operator, mixed, precision=lax.Precision.HIGHEST)
    atm_next = mixed + 0.25 * lateral
    atm_next = atm_next.at[2, 0].add(0.5 * temp_in)
    ocean_next = vertical(ocean_state, ocean_mixing)
    ocean_next = ocean_next.at[0, 0].add(0.5 * heat_in)
    return atm_next, ocean_next
```

```python
import jax
import jax.numpy as jnp
from jax import lax
from jax.experimental import pallas as pl
from jax.experimental.pallas import tpu as pltpu
from jax.sharding import PartitionSpec as P

BLOCK = 128
NEAR = 2
CAP = 2
REACH = 2 * NEAR + 1
LANE = {0: 1, 1: 2, 2: 0, 3: 3, 4: 4}
EMPTY = 64


def prep_kernel(
    ocean_src, ocean_dst, atmos_src, atmos_dst,
    atm, ocean, flux, sea, ocean_tiles, atmos_tiles,
    send, up, down, picks,
):
    level = lax.axis_index("lev")
    picks[0:16] = flux[:, 0:128].astype(jnp.float32)
    picks[16:32] = flux[:, 128:256].astype(jnp.float32)
    picks[32:64] = sea[...].astype(jnp.float32)
    send[...] = jnp.zeros_like(send)
    for slot in range(REACH * CAP):
        reach, place = slot // CAP, slot % CAP
        base = 8 * LANE[reach]
        source = ocean_src[slot]
        row = picks[pl.ds((source % 2) * 16 + source // 2, 1), :].astype(jnp.bfloat16)
        product = lax.dot_general(
            row, ocean_tiles[slot], (((1,), (1,)), ((), ())), preferred_element_type=jnp.float32
        )
        send[base + place : base + place + 1] = product.astype(jnp.bfloat16).astype(jnp.float32)
        source = atmos_src[slot]
        row = picks[pl.ds(32 + source, 1), :].astype(jnp.bfloat16)
        product = lax.dot_general(
            row, atmos_tiles[slot], (((1,), (1,)), ((), ())), preferred_element_type=jnp.float32
        )
        send[base + 2 + place : base + 3 + place] = product.astype(jnp.bfloat16).astype(jnp.float32)
    lane = lax.broadcasted_iota(jnp.int32, (4, 128), 1)
    line = lax.broadcasted_iota(jnp.int32, (4, 128), 0)
    inside = lane % 64 - 8 * level
    codes = jnp.where((inside >= 4) & (inside < 8), EMPTY, 0)
    for slot in range(REACH * CAP):
        reach, place = slot // CAP, slot % CAP
        here = (line == reach // 2) & (lane // 64 == reach % 2)
        to = ocean_dst[slot]
        codes = jnp.where(here & (inside == place), jnp.where(to < 32, to, EMPTY), codes)
        to = atmos_dst[slot]
        code = jnp.where(to < 32, 32 + (to % 2) * 16 + to // 2, EMPTY)
        codes = jnp.where(here & (inside == 2 + place), code, codes)
    send[4:8] = codes.astype(jnp.float32)
    for field in range(4):
        rows = slice(16 * field, 16 * field + 16)
        more = slice(64 + 16 * field, 80 + 16 * field)
        up[rows] = atm[field, 1, :, 0:128]
        up[more] = atm[field, 1, :, 128:256]
        down[rows] = atm[field, 0, :, 0:128]
        down[more] = atm[field, 0, :, 128:256]
    down[128:192] = ocean[pl.ds(0, 64, stride=2), :]
    up[128:192] = ocean[pl.ds(1, 64, stride=2), :]


def final_kernel(
    atm_mixing, ocean_mixing,
    atm, ocean, operator, below, above, own, in0, in1, in3, in4,
    atm_out, ocean_out,
):
    level = lax.axis_index("lev")
    last = lax.axis_size("lev") - 1
    at_bottom = level == 0
    at_top = level == last
    for field in range(4):
        low, high = atm[field, 0], atm[field, 1]
        rows = slice(16 * field, 16 * field + 16)
        more = slice(64 + 16 * field, 80 + 16 * field)
        beneath = jnp.where(at_bottom, low, jnp.concatenate([below[rows], below[more]], axis=1))
        overhead = jnp.where(at_top, high, jnp.concatenate([above[rows], above[more]], axis=1))
        mixed_low = low + atm_mixing[field, 0] * (high - 2.0 * low + beneath)
        mixed_high = high + atm_mixing[field, 1] * (overhead - 2.0 * high + low)
        mixed = jnp.concatenate([mixed_low, mixed_high], axis=1)
        lateral = jnp.dot(
            operator[...], mixed, precision=lax.Precision.HIGHEST, preferred_element_type=jnp.float32
        )
        result = mixed + 0.25 * lateral
        atm_out[field, 0] = result[:, 0:256]
        atm_out[field, 1] = result[:, 256:512]
    for field in range(2):
        low = ocean[pl.ds(64 * field, 32, stride=2), :]
        high = ocean[pl.ds(64 * field + 1, 32, stride=2), :]
        rows = slice(128 + 32 * field, 160 + 32 * field)
        beneath = jnp.where(at_bottom, low, below[rows])
        overhead = jnp.where(at_top, high, above[rows])
        ocean_out[pl.ds(64 * field, 32, stride=2), :] = low + ocean_mixing[field, 0] * (
            high - 2.0 * low + beneath
        )
        ocean_out[pl.ds(64 * field + 1, 32, stride=2), :] = high + ocean_mixing[field, 1] * (
            overhead - 2.0 * high + low
        )

    @pl.when(at_bottom)
    def _():
        codes = own[4:8]
        for source in range(1, 8):
            codes = codes + own[8 * source + 4 : 8 * source + 8]
        labels = lax.broadcasted_iota(jnp.int32, (64, 64), 0).astype(jnp.float32)
        total = jnp.zeros((64, 128), jnp.float32)
        for reach, inbound in enumerate((in0, in1, own, in3, in4)):
            to = codes[reach // 2 : reach // 2 + 1, 64 * (reach % 2) : 64 * (reach % 2) + 64]
            onehot = (to == labels).astype(jnp.float32).astype(jnp.bfloat16)
            total = total + jnp.dot(
                onehot, inbound[...].astype(jnp.bfloat16), preferred_element_type=jnp.float32
            )
        total = 0.5 * total
        even = ocean_out[pl.ds(0, 32, stride=2), :]
        ocean_out[pl.ds(0, 32, stride=2), :] = even + total[0:32]
        atm_out[2, 0, :, 0:128] = atm_out[2, 0, :, 0:128] + total[32:48]
        atm_out[2, 0, :, 128:256] = atm_out[2, 0, :, 128:256] + total[48:64]


def shards(
    atm_state,
    atm_mixing,
    element_operator,
    ocean_state,
    ocean_mixing,
    atm_flux,
    sea_temp,
    ocean_tiles,
    ocean_tile_src,
    ocean_tile_dst,
    atmos_tiles,
    atmos_tile_src,
    atmos_tile_dst,
):
    columns, levels = lax.axis_size("horiz"), lax.axis_size("lev")
    f32 = jnp.float32
    smem = pl.BlockSpec(memory_space=pltpu.SMEM)
    vmem = pl.BlockSpec(memory_space=pltpu.VMEM)
    ocean_rows = ocean_state.reshape(2, 2, 32, 128).transpose(0, 2, 1, 3).reshape(128, 128)
    send, up, down = pl.pallas_call(
        prep_kernel,
        out_shape=(
            jax.ShapeDtypeStruct((64, 128), f32),
            jax.ShapeDtypeStruct((192, 128), f32),
            jax.ShapeDtypeStruct((192, 128), f32),
        ),
        in_specs=[smem] * 4 + [vmem] * 6,
        out_specs=(vmem, vmem, vmem),
        scratch_shapes=[pltpu.VMEM((64, 128), f32)],
        compiler_params=pltpu.CompilerParams(vmem_limit_bytes=8 << 20),
    )(
        ocean_tile_src, ocean_tile_dst, atmos_tile_src, atmos_tile_dst,
        atm_state, ocean_rows, atm_flux, sea_temp.reshape(32, 128), ocean_tiles, atmos_tiles,
    )
    own = lax.all_to_all(send, "lev", 0, 0, tiled=True)
    own, up, down = lax.optimization_barrier((own, up, down))

    def to_owner(reach):
        step = reach - NEAR
        pairs = [
            (h * levels + LANE[reach], ((h + step) % columns) * levels) for h in range(columns)
        ]
        return lax.ppermute(own, ("horiz", "lev"), pairs)

    inbound = [to_owner(reach) for reach in (0, 1, 3, 4)]
    below = lax.ppermute(up, "lev", [(i, i + 1) for i in range(levels - 1)])
    above = lax.ppermute(down, "lev", [(i + 1, i) for i in range(levels - 1)])
    atm_next, ocean_next = pl.pallas_call(
        final_kernel,
        out_shape=(
            jax.ShapeDtypeStruct(atm_state.shape, f32),
            jax.ShapeDtypeStruct((128, 128), f32),
        ),
        in_specs=[smem] * 2 + [vmem] * 10,
        out_specs=(vmem, vmem),
        compiler_params=pltpu.CompilerParams(vmem_limit_bytes=8 << 20),
    )(
        atm_mixing, ocean_mixing, atm_state, ocean_rows, element_operator,
        below, above, own, *inbound,
    )
    ocean_next = ocean_next.reshape(2, 32, 2, 128).transpose(0, 2, 1, 3).reshape(ocean_state.shape)
    return (atm_next, ocean_next)


def solution(mesh):
    placed = (
        P(None, "lev", None, "horiz"),
        P(None, "lev"),
        P(),
        P(None, "lev", "horiz"),
        P(None, "lev"),
        P(None, "horiz"),
        P("horiz"),
        P(("horiz", "lev"), None, None),
        P(("horiz", "lev")),
        P(("horiz", "lev")),
        P(("horiz", "lev"), None, None),
        P(("horiz", "lev")),
        P(("horiz", "lev")),
    )
    return jax.shard_map(
        shards,
        mesh=mesh,
        in_specs=placed,
        out_specs=(P(None, "lev", None, "horiz"), P(None, "lev", "horiz")),
        check_vma=False,
    )
```

```python
import jax
import jax.numpy as jnp
from jax import lax
from jax.experimental import pallas as pl
from jax.experimental.pallas import tpu as pltpu
from jax.sharding import PartitionSpec as P

BLOCK = 128
NEAR = 2
CAP = 2
REACH = 2 * NEAR + 1
NEXT = ((0, 2), (0, 1))
PREVIOUS = ((1, 6), (1, 1))
EMPTY = 64


def prep_kernel(
    ocean_src_hbm, ocean_dst_hbm, atmos_src_hbm, atmos_dst_hbm,
    atm_hbm, ocean_hbm, flux_hbm, sea_hbm, ocean_tiles_hbm, atmos_tiles_hbm,
    send, up, down,
    ocean_src, ocean_dst, atmos_src, atmos_dst, ocean, flux, sea, ocean_tiles, atmos_tiles, picks, rows_out, sems,
):
    level = lax.axis_index("lev")
    odd = lax.axis_index("horiz") % 2
    moves = [
        (flux_hbm, flux), (sea_hbm, sea), (ocean_src_hbm, ocean_src), (atmos_src_hbm, atmos_src),
        (ocean_dst_hbm, ocean_dst), (atmos_dst_hbm, atmos_dst),
        (ocean_tiles_hbm, ocean_tiles), (atmos_tiles_hbm, atmos_tiles),
        (ocean_hbm, ocean),
        (atm_hbm.at[:, 1, :, 0:128], up.at[0:4]), (atm_hbm.at[:, 1, :, 128:256], up.at[4:8]),
        (atm_hbm.at[:, 0, :, 0:128], down.at[0:4]), (atm_hbm.at[:, 0, :, 128:256], down.at[4:8]),
    ]
    copies = [
        pltpu.make_async_copy(source, target, sems.at[i]) for i, (source, target) in enumerate(moves)
    ]
    for copy in copies:
        copy.start()
    rows_out[...] = jnp.zeros_like(rows_out)
    for copy in copies[0:6]:
        copy.wait()
    lane = lax.broadcasted_iota(jnp.int32, (4, 128), 1)
    line = lax.broadcasted_iota(jnp.int32, (4, 128), 0)
    inside = lane % 64 - 8 * level
    codes = jnp.where((inside >= 0) & (inside < 8), EMPTY, 0)
    for reach in range(REACH):
        delta = reach - NEAR
        array_even, from_even = (0, -delta) if -delta in (0, 1) else (1, 2 - delta) if delta > 0 else (2, -delta - 2)
        array_odd, from_odd = (0, 1 - delta) if 1 - delta in (0, 1) else (1, 3 - delta) if delta > 0 else (2, -delta - 1)
        here = (line == jnp.where(odd == 0, array_even, array_odd)) & (
            lane // 64 == jnp.where(odd == 0, from_even, from_odd)
        )
        for place in range(CAP):
            to = ocean_dst[reach * CAP + place]
            codes = jnp.where(here & (inside == place), jnp.where(to < 32, to, EMPTY), codes)
            to = atmos_dst[reach * CAP + place]
            code = jnp.where(to < 32, 32 + (to % 2) * 16 + to // 2, EMPTY)
            codes = jnp.where(here & (inside == CAP + place), code, codes)
    rows_out[pl.ds(64 * odd + 4, 4), :] = codes.astype(jnp.float32)
    picks[0:16] = flux[:, 0:128].astype(jnp.float32)
    picks[16:32] = flux[:, 128:256].astype(jnp.float32)
    picks[32:64] = sea[...].astype(jnp.float32)

    def product(row, tile):
        return lax.dot_general(
            row.astype(jnp.bfloat16), tile, (((1,), (1,)), ((), ())), preferred_element_type=jnp.float32
        ).astype(jnp.bfloat16).astype(jnp.float32)

    def chunk(reach):
        def member(target):
            column, lev = PREVIOUS[target + 2] if target < 0 else NEXT[target - 2] if target > 1 else (target, 0)
            return column * 8 + lev

        return 8 * jnp.where(odd == 0, member(reach - NEAR), member(reach - NEAR + 1))

    copies[6].wait()
    for slot in range(REACH * CAP):
        source = ocean_src[slot]
        row = picks[pl.ds((source % 2) * 16 + source // 2, 1), :]
        rows_out[pl.ds(chunk(slot // CAP) + slot % CAP, 1), :] = product(row, ocean_tiles[slot])
    copies[7].wait()
    for slot in range(REACH * CAP):
        row = picks[pl.ds(32 + atmos_src[slot], 1), :]
        rows_out[pl.ds(chunk(slot // CAP) + CAP + slot % CAP, 1), :] = product(row, atmos_tiles[slot])
    send[...] = rows_out[...].astype(jnp.bfloat16)
    copies[8].wait()
    down[8:12] = ocean[pl.ds(0, 64, stride=2), :].reshape(4, 16, 128)
    up[8:12] = ocean[pl.ds(1, 64, stride=2), :].reshape(4, 16, 128)
    for copy in copies[9:]:
        copy.wait()


def column_kernel(
    atm_mixing, ocean_mixing, atm, ocean, operator, below, above,
    atm_hbm, ocean_hbm, atm_base, ocean_base,
    atm_out, ocean_out, sems,
):
    level = lax.axis_index("lev")
    at_bottom = level == 0
    at_top = level == lax.axis_size("lev") - 1
    for field in range(2):
        low = ocean[pl.ds(64 * field, 32, stride=2), :]
        high = ocean[pl.ds(64 * field + 1, 32, stride=2), :]
        beneath = jnp.where(at_bottom, low, below[8 + 2 * field : 10 + 2 * field].reshape(32, 128))
        overhead = jnp.where(at_top, high, above[8 + 2 * field : 10 + 2 * field].reshape(32, 128))
        ocean_out[pl.ds(64 * field, 32, stride=2), :] = low + ocean_mixing[field, 0] * (
            high - 2.0 * low + beneath
        )
        ocean_out[pl.ds(64 * field + 1, 32, stride=2), :] = high + ocean_mixing[field, 1] * (
            overhead - 2.0 * high + low
        )
    ocean_copy = pltpu.make_async_copy(ocean_out, ocean_hbm, sems.at[0])
    ocean_copy.start()
    ocean_base[...] = ocean_out[0:64]
    for field in range(4):
        low, high = atm[field, 0], atm[field, 1]
        beneath = jnp.where(at_bottom, low, jnp.concatenate([below[field], below[4 + field]], axis=1))
        overhead = jnp.where(at_top, high, jnp.concatenate([above[field], above[4 + field]], axis=1))
        mixed_low = low + atm_mixing[0, field] * (high - 2.0 * low + beneath)
        mixed_high = high + atm_mixing[1, field] * (overhead - 2.0 * high + low)
        mixed = jnp.concatenate([mixed_low, mixed_high], axis=1)
        lateral = jnp.dot(
            operator[...], mixed, precision=lax.Precision.HIGHEST, preferred_element_type=jnp.float32
        )
        result = mixed + 0.25 * lateral
        atm_out[field, 0] = result[:, 0:256]
        atm_out[field, 1] = result[:, 256:512]
    atm_copy = pltpu.make_async_copy(atm_out, atm_hbm, sems.at[1])
    atm_copy.start()
    atm_base[...] = atm_out[2, 0]
    ocean_copy.wait()
    atm_copy.wait()


def surface_kernel(
    atm_in, ocean_in, atm_base, ocean_base, own, previous, following,
    atm_hbm, ocean_hbm,
    atm_rows, ocean_rows, sems,
):
    del atm_in, ocean_in

    @pl.when(lax.axis_index("lev") == 0)
    def _():
        codes = jnp.sum(own[...].astype(jnp.float32).reshape(16, 8, 128), axis=0)
        labels = lax.broadcasted_iota(jnp.int32, (64, 128), 0).astype(jnp.float32)
        total = jnp.zeros((64, 128), jnp.float32)
        for i, inbound in enumerate((own, previous, following)):
            onehot = jnp.where(codes[4 + i : 5 + i] == labels, 1.0, 0.0).astype(jnp.bfloat16)
            total = total + jnp.dot(onehot, inbound[...], preferred_element_type=jnp.float32)
        total = 0.5 * total
        ocean_rows[...] = ocean_base[...]
        ocean_rows[pl.ds(0, 32, stride=2), :] = ocean_base[pl.ds(0, 32, stride=2), :] + total[0:32]
        ocean_copy = pltpu.make_async_copy(ocean_rows, ocean_hbm.at[0:64], sems.at[0])
        ocean_copy.start()
        atm_rows[:, 0:128] = atm_base[:, 0:128] + total[32:48]
        atm_rows[:, 128:256] = atm_base[:, 128:256] + total[48:64]
        atm_copy = pltpu.make_async_copy(atm_rows, atm_hbm.at[2, 0], sems.at[1])
        atm_copy.start()
        ocean_copy.wait()
        atm_copy.wait()


def shards(
    atm_state,
    atm_mixing,
    element_operator,
    ocean_state,
    ocean_mixing,
    atm_flux,
    sea_temp,
    ocean_tiles,
    ocean_tile_src,
    ocean_tile_dst,
    atmos_tiles,
    atmos_tile_src,
    atmos_tile_dst,
):
    columns, levels = lax.axis_size("horiz"), lax.axis_size("lev")
    f32, bf16 = jnp.float32, jnp.bfloat16
    vmem = pl.BlockSpec(memory_space=pltpu.VMEM)
    hbm = pl.BlockSpec(memory_space=pltpu.HBM)
    smem = pl.BlockSpec(memory_space=pltpu.SMEM)
    shape = jax.ShapeDtypeStruct
    params = pltpu.CompilerParams(vmem_limit_bytes=8 << 20)
    whole = pltpu.CompilerParams(vmem_limit_bytes=61 << 20)
    ocean_rows = ocean_state.reshape(2, 2, 32, 128).transpose(0, 2, 1, 3).reshape(128, 128)
    send, up, down = pl.pallas_call(
        prep_kernel,
        out_shape=(
            shape((128, 128), bf16),
            shape((12, 16, 128), f32),
            shape((12, 16, 128), f32),
        ),
        in_specs=[hbm] * 10,
        out_specs=(vmem,) * 3,
        scratch_shapes=[pltpu.SMEM((REACH * CAP,), jnp.int32)] * 4
        + [
            pltpu.VMEM((128, 128), f32),
            pltpu.VMEM((16, 256), bf16),
            pltpu.VMEM((32, 128), bf16),
            pltpu.VMEM((REACH * CAP, BLOCK, BLOCK), bf16),
            pltpu.VMEM((REACH * CAP, BLOCK, BLOCK), bf16),
            pltpu.VMEM((64, 128), f32),
            pltpu.VMEM((128, 128), f32),
            pltpu.SemaphoreType.DMA((13,)),
        ],
        compiler_params=whole,
    )(
        ocean_tile_src, ocean_tile_dst, atmos_tile_src, atmos_tile_dst,
        atm_state, ocean_rows, atm_flux, sea_temp.reshape(32, 128), ocean_tiles, atmos_tiles,
    )
    pairs = [[h * levels + l for h in (g, g + 1) for l in range(levels)] for g in range(0, columns, 2)]
    own = lax.all_to_all(send, ("horiz", "lev"), 0, 0, axis_index_groups=pairs, tiled=True)

    def to_owner(lanes, step):
        return lax.ppermute(
            own,
            ("horiz", "lev"),
            [
                ((g + column) * levels + lev, (g + step + i) % columns * levels)
                for g in range(0, columns, 2)
                for i, (column, lev) in enumerate(lanes)
            ],
        )

    previous = to_owner(NEXT, 2)
    following = to_owner(PREVIOUS, -2)
    below = lax.ppermute(up, "lev", [(i, i + 1) for i in range(levels - 1)])
    above = lax.ppermute(down, "lev", [(i + 1, i) for i in range(levels - 1)])
    atm_next, ocean_next, atm_base, ocean_base = pl.pallas_call(
        column_kernel,
        out_shape=(
            shape(atm_state.shape, f32),
            shape((128, 128), f32),
            shape((16, 256), f32),
            shape((64, 128), f32),
        ),
        in_specs=[smem] * 2 + [vmem] * 5,
        out_specs=(hbm, hbm, vmem, vmem),
        scratch_shapes=[
            pltpu.VMEM(atm_state.shape, f32),
            pltpu.VMEM((128, 128), f32),
            pltpu.SemaphoreType.DMA((2,)),
        ],
        compiler_params=params,
    )(atm_mixing.T, ocean_mixing, atm_state, ocean_rows, element_operator, below, above)
    atm_next, ocean_next = pl.pallas_call(
        surface_kernel,
        out_shape=(shape(atm_state.shape, f32), shape((128, 128), f32)),
        in_specs=[hbm] * 2 + [vmem] * 5,
        out_specs=(hbm, hbm),
        scratch_shapes=[
            pltpu.VMEM((16, 256), f32),
            pltpu.VMEM((64, 128), f32),
            pltpu.SemaphoreType.DMA((2,)),
        ],
        input_output_aliases={0: 0, 1: 1},
        compiler_params=params,
    )(atm_next, ocean_next, atm_base, ocean_base, own, previous, following)
    ocean_next = ocean_next.reshape(2, 32, 2, 128).transpose(0, 2, 1, 3).reshape(ocean_state.shape)
    return (atm_next, ocean_next)


def solution(mesh):
    placed = (
        P(None, "lev", None, "horiz"),
        P(None, "lev"),
        P(),
        P(None, "lev", "horiz"),
        P(None, "lev"),
        P(None, "horiz"),
        P("horiz"),
        P(("horiz", "lev"), None, None),
        P(("horiz", "lev")),
        P(("horiz", "lev")),
        P(("horiz", "lev"), None, None),
        P(("horiz", "lev")),
        P(("horiz", "lev")),
    )
    return jax.shard_map(
        shards,
        mesh=mesh,
        in_specs=placed,
        out_specs=(P(None, "lev", None, "horiz"), P(None, "lev", "horiz")),
        check_vma=False,
    )
```

```python
import jax
import jax.numpy as jnp
from jax import lax
from jax.experimental import pallas as pl
from jax.experimental.pallas import tpu as pltpu
from jax.sharding import PartitionSpec as P

BLOCK = 128
NEAR = 2
CAP = 2
REACH = 2 * NEAR + 1
NEXT = ((0, 1), (1, 1))
PREVIOUS = ((1, 6), (1, 2))
EMPTY = 64


def prep_kernel(
    ocean_src_hbm, ocean_dst_hbm, atmos_src_hbm, atmos_dst_hbm,
    atm_hbm, ocean_hbm, flux_hbm, sea_hbm, ocean_tiles_hbm, atmos_tiles_hbm,
    send, up, down,
    ocean_src, ocean_dst, atmos_src, atmos_dst, ocean, flux, sea, ocean_tiles, atmos_tiles, picks, rows_out, sems,
):
    level = lax.axis_index("lev")
    odd = lax.axis_index("horiz") % 2
    odd_pair = lax.axis_index("horiz") // 2 % 2
    moves = [
        (flux_hbm, flux), (sea_hbm, sea), (ocean_src_hbm, ocean_src), (atmos_src_hbm, atmos_src),
        (ocean_dst_hbm, ocean_dst), (atmos_dst_hbm, atmos_dst),
        (ocean_tiles_hbm, ocean_tiles), (atmos_tiles_hbm, atmos_tiles),
        (ocean_hbm, ocean),
        (atm_hbm.at[:, 1, :, 0:128], up.at[0:4]), (atm_hbm.at[:, 1, :, 128:256], up.at[4:8]),
        (atm_hbm.at[:, 0, :, 0:128], down.at[0:4]), (atm_hbm.at[:, 0, :, 128:256], down.at[4:8]),
    ]
    copies = [
        pltpu.make_async_copy(source, target, sems.at[i]) for i, (source, target) in enumerate(moves)
    ]
    for copy in copies:
        copy.start()
    rows_out[...] = jnp.zeros_like(rows_out)
    for copy in copies[0:6]:
        copy.wait()
    lane = lax.broadcasted_iota(jnp.int32, (4, 128), 1)
    line = lax.broadcasted_iota(jnp.int32, (4, 128), 0)
    inside = lane % 64 - 8 * level
    codes = jnp.where((inside >= 0) & (inside < 8), EMPTY, 0)
    for reach in range(REACH):
        delta = reach - NEAR
        array_even, from_even = (0, -delta) if -delta in (0, 1) else (1, 2 - delta) if delta > 0 else (2, -delta - 2)
        array_odd, from_odd = (0, 1 - delta) if 1 - delta in (0, 1) else (1, 3 - delta) if delta > 0 else (2, -delta - 1)
        array = jnp.where(odd == 0, array_even, array_odd)
        here = (line == jnp.where((odd_pair == 1) & (array > 0), 3 - array, array)) & (
            lane // 64 == jnp.where(odd == 0, from_even, from_odd)
        )
        for place in range(CAP):
            to = ocean_dst[reach * CAP + place]
            codes = jnp.where(here & (inside == place), jnp.where(to < 32, to, EMPTY), codes)
            to = atmos_dst[reach * CAP + place]
            code = jnp.where(to < 32, 32 + (to % 2) * 16 + to // 2, EMPTY)
            codes = jnp.where(here & (inside == CAP + place), code, codes)
    rows_out[pl.ds(64 * odd + 4, 4), :] = codes.astype(jnp.float32)
    picks[0:16] = flux[:, 0:128].astype(jnp.float32)
    picks[16:32] = flux[:, 128:256].astype(jnp.float32)
    picks[32:64] = sea[...].astype(jnp.float32)

    def product(row, tile):
        return lax.dot_general(
            row.astype(jnp.bfloat16), tile, (((1,), (1,)), ((), ())), preferred_element_type=jnp.float32
        ).astype(jnp.bfloat16).astype(jnp.float32)

    def chunk(reach):
        def member(target):
            column, lev = PREVIOUS[target + 2] if target < 0 else NEXT[target - 2] if target > 1 else (target, 0)
            return column * 8 + lev

        return 8 * jnp.where(odd == 0, member(reach - NEAR), member(reach - NEAR + 1))

    copies[8].wait()
    down[8:12] = ocean[pl.ds(0, 64, stride=2), :].reshape(4, 16, 128)
    up[8:12] = ocean[pl.ds(1, 64, stride=2), :].reshape(4, 16, 128)
    copies[6].wait()
    for slot in range(REACH * CAP):
        source = ocean_src[slot]
        row = picks[pl.ds((source % 2) * 16 + source // 2, 1), :]
        rows_out[pl.ds(chunk(slot // CAP) + slot % CAP, 1), :] = product(row, ocean_tiles[slot])
    copies[7].wait()
    for slot in range(REACH * CAP):
        row = picks[pl.ds(32 + atmos_src[slot], 1), :]
        rows_out[pl.ds(chunk(slot // CAP) + CAP + slot % CAP, 1), :] = product(row, atmos_tiles[slot])
    send[...] = rows_out[...].astype(jnp.bfloat16)
    for copy in copies[9:]:
        copy.wait()


def column_kernel(
    atm_mixing, ocean_mixing, atm, ocean, operator, below, above,
    atm_hbm, ocean_hbm, atm_base, ocean_base,
    atm_out, ocean_out, sems,
):
    level = lax.axis_index("lev")
    at_bottom = level == 0
    at_top = level == lax.axis_size("lev") - 1
    for field in range(2):
        low = ocean[pl.ds(64 * field, 32, stride=2), :]
        high = ocean[pl.ds(64 * field + 1, 32, stride=2), :]
        beneath = jnp.where(at_bottom, low, below[8 + 2 * field : 10 + 2 * field].reshape(32, 128))
        overhead = jnp.where(at_top, high, above[8 + 2 * field : 10 + 2 * field].reshape(32, 128))
        ocean_out[pl.ds(64 * field, 32, stride=2), :] = low + ocean_mixing[field : field + 1, 0:1] * (
            high - 2.0 * low + beneath
        )
        ocean_out[pl.ds(64 * field + 1, 32, stride=2), :] = high + ocean_mixing[field : field + 1, 1:2] * (
            overhead - 2.0 * high + low
        )
    ocean_copy = pltpu.make_async_copy(ocean_out, ocean_hbm, sems.at[0])
    ocean_copy.start()
    ocean_base[...] = ocean_out[0:64]
    for field in range(4):
        low, high = atm[field, 0], atm[field, 1]
        beneath = jnp.where(at_bottom, low, jnp.concatenate([below[field], below[4 + field]], axis=1))
        overhead = jnp.where(at_top, high, jnp.concatenate([above[field], above[4 + field]], axis=1))
        mixed_low = low + atm_mixing[0:1, field : field + 1] * (high - 2.0 * low + beneath)
        mixed_high = high + atm_mixing[1:2, field : field + 1] * (overhead - 2.0 * high + low)
        mixed = jnp.concatenate([mixed_low, mixed_high], axis=1)
        lateral = jnp.dot(
            operator[...], mixed, precision=lax.Precision.HIGHEST, preferred_element_type=jnp.float32
        )
        result = mixed + 0.25 * lateral
        atm_out[field, 0] = result[:, 0:256]
        atm_out[field, 1] = result[:, 256:512]
    atm_copy = pltpu.make_async_copy(atm_out, atm_hbm, sems.at[1])
    atm_copy.start()
    atm_base[...] = atm_out[2, 0]
    ocean_copy.wait()
    atm_copy.wait()


def surface_kernel(
    atm_in, ocean_in, atm_base, ocean_base, own, second, first,
    atm_hbm, ocean_hbm,
    atm_rows, ocean_rows, sems,
):
    del atm_in, ocean_in

    @pl.when(lax.axis_index("lev") == 0)
    def _():
        codes = jnp.sum(own[...].astype(jnp.float32).reshape(16, 8, 128), axis=0)
        labels = lax.broadcasted_iota(jnp.int32, (64, 128), 0).astype(jnp.float32)
        total = jnp.zeros((64, 128), jnp.float32)
        for i, inbound in enumerate((own, first, second)):
            onehot = jnp.where(codes[4 + i : 5 + i] == labels, 1.0, 0.0).astype(jnp.bfloat16)
            total = total + jnp.dot(onehot, inbound[...], preferred_element_type=jnp.float32)
        total = 0.5 * total
        ocean_rows[...] = ocean_base[...]
        ocean_rows[pl.ds(0, 32, stride=2), :] = ocean_base[pl.ds(0, 32, stride=2), :] + total[0:32]
        ocean_copy = pltpu.make_async_copy(ocean_rows, ocean_hbm.at[0:64], sems.at[0])
        ocean_copy.start()
        atm_rows[:, 0:128] = atm_base[:, 0:128] + total[32:48]
        atm_rows[:, 128:256] = atm_base[:, 128:256] + total[48:64]
        atm_copy = pltpu.make_async_copy(atm_rows, atm_hbm.at[2, 0], sems.at[1])
        atm_copy.start()
        ocean_copy.wait()
        atm_copy.wait()


def shards(
    atm_state,
    atm_mixing,
    element_operator,
    ocean_state,
    ocean_mixing,
    atm_flux,
    sea_temp,
    ocean_tiles,
    ocean_tile_src,
    ocean_tile_dst,
    atmos_tiles,
    atmos_tile_src,
    atmos_tile_dst,
):
    columns, levels = lax.axis_size("horiz"), lax.axis_size("lev")
    f32, bf16 = jnp.float32, jnp.bfloat16
    vmem = pl.BlockSpec(memory_space=pltpu.VMEM)
    hbm = pl.BlockSpec(memory_space=pltpu.HBM)
    shape = jax.ShapeDtypeStruct
    params = pltpu.CompilerParams(vmem_limit_bytes=8 << 20)
    whole = pltpu.CompilerParams(vmem_limit_bytes=61 << 20)
    ocean_rows = ocean_state.reshape(2, 2, 32, 128).transpose(0, 2, 1, 3).reshape(128, 128)
    send, up, down = pl.pallas_call(
        prep_kernel,
        out_shape=(
            shape((128, 128), bf16),
            shape((12, 16, 128), f32),
            shape((12, 16, 128), f32),
        ),
        in_specs=[hbm] * 10,
        out_specs=(vmem,) * 3,
        scratch_shapes=[pltpu.SMEM((REACH * CAP,), jnp.int32)] * 4
        + [
            pltpu.VMEM((128, 128), f32),
            pltpu.VMEM((16, 256), bf16),
            pltpu.VMEM((32, 128), bf16),
            pltpu.VMEM((REACH * CAP, BLOCK, BLOCK), bf16),
            pltpu.VMEM((REACH * CAP, BLOCK, BLOCK), bf16),
            pltpu.VMEM((64, 128), f32),
            pltpu.VMEM((128, 128), f32),
            pltpu.SemaphoreType.DMA((13,)),
        ],
        compiler_params=whole,
    )(
        ocean_tile_src, ocean_tile_dst, atmos_tile_src, atmos_tile_dst,
        atm_state, ocean_rows, atm_flux, sea_temp.reshape(32, 128), ocean_tiles, atmos_tiles,
    )
    pairs = [[h * levels + l for h in (g, g + 1) for l in range(levels)] for g in range(0, columns, 2)]
    own = lax.all_to_all(send, ("horiz", "lev"), 0, 0, axis_index_groups=pairs, tiled=True)

    def swap(wave):
        pairs = []
        for g in range(2 - 2 * wave, columns, 4):
            for i in range(2):
                column, lev = NEXT[i]
                pairs.append(((g + column) * levels + lev, (g + 2 + i) % columns * levels))
                column, lev = PREVIOUS[i]
                pairs.append((((g + 2) % columns + column) * levels + lev, (g + i) * levels))
        return lax.ppermute(own, ("horiz", "lev"), pairs)

    second = swap(1)
    first = swap(0)
    below = lax.ppermute(up, "lev", [(i, i + 1) for i in range(levels - 1)])
    above = lax.ppermute(down, "lev", [(i + 1, i) for i in range(levels - 1)])
    atm_next, ocean_next, atm_base, ocean_base = pl.pallas_call(
        column_kernel,
        out_shape=(
            shape(atm_state.shape, f32),
            shape((128, 128), f32),
            shape((16, 256), f32),
            shape((64, 128), f32),
        ),
        in_specs=[vmem] * 7,
        out_specs=(hbm, hbm, vmem, vmem),
        scratch_shapes=[
            pltpu.VMEM(atm_state.shape, f32),
            pltpu.VMEM((128, 128), f32),
            pltpu.SemaphoreType.DMA((2,)),
        ],
        compiler_params=params,
    )(atm_mixing.T, ocean_mixing, atm_state, ocean_rows, element_operator, below, above)
    atm_next, ocean_next = pl.pallas_call(
        surface_kernel,
        out_shape=(shape(atm_state.shape, f32), shape((128, 128), f32)),
        in_specs=[hbm] * 2 + [vmem] * 5,
        out_specs=(hbm, hbm),
        scratch_shapes=[
            pltpu.VMEM((16, 256), f32),
            pltpu.VMEM((64, 128), f32),
            pltpu.SemaphoreType.DMA((2,)),
        ],
        input_output_aliases={0: 0, 1: 1},
        compiler_params=params,
    )(atm_next, ocean_next, atm_base, ocean_base, own, second, first)
    ocean_next = ocean_next.reshape(2, 32, 2, 128).transpose(0, 2, 1, 3).reshape(ocean_state.shape)
    return (atm_next, ocean_next)


def solution(mesh):
    placed = (
        P(None, "lev", None, "horiz"),
        P(None, "lev"),
        P(),
        P(None, "lev", "horiz"),
        P(None, "lev"),
        P(None, "horiz"),
        P("horiz"),
        P(("horiz", "lev"), None, None),
        P(("horiz", "lev")),
        P(("horiz", "lev")),
        P(("horiz", "lev"), None, None),
        P(("horiz", "lev")),
        P(("horiz", "lev")),
    )
    return jax.shard_map(
        shards,
        mesh=mesh,
        in_specs=placed,
        out_specs=(P(None, "lev", None, "horiz"), P(None, "lev", "horiz")),
        check_vma=False,
    )
```

```python
import jax
import jax.numpy as jnp
from jax import lax
from jax.experimental import pallas as pl
from jax.experimental.pallas import tpu as pltpu
from jax.sharding import PartitionSpec as P

BLOCK = 128
NEAR = 2
CAP = 2
REACH = 2 * NEAR + 1
NEXT = ((0, 1), (1, 1))
PREVIOUS = ((1, 6), (1, 2))
EMPTY = 64


def seat(level):
    return 7 - level


def prep_kernel(
    ocean_src_hbm, ocean_dst_hbm, atmos_src_hbm, atmos_dst_hbm,
    atm_hbm, ocean_hbm, flux_hbm, sea_hbm, ocean_tiles_hbm, atmos_tiles_hbm,
    send, up, down,
    ocean_src, ocean_dst, atmos_src, atmos_dst, ocean, flux, sea, ocean_tiles, atmos_tiles, picks, rows_out, sems,
):
    level = lax.axis_index("lev")
    odd = lax.axis_index("horiz") % 2
    odd_pair = lax.axis_index("horiz") // 2 % 2
    moves = [
        (flux_hbm, flux), (sea_hbm, sea), (ocean_src_hbm, ocean_src), (atmos_src_hbm, atmos_src),
        (ocean_dst_hbm, ocean_dst), (atmos_dst_hbm, atmos_dst),
        (ocean_tiles_hbm, ocean_tiles), (atmos_tiles_hbm, atmos_tiles),
        (ocean_hbm, ocean),
        (atm_hbm.at[:, 1, :, 0:128], up.at[0:4]), (atm_hbm.at[:, 1, :, 128:256], up.at[4:8]),
        (atm_hbm.at[:, 0, :, 0:128], down.at[0:4]), (atm_hbm.at[:, 0, :, 128:256], down.at[4:8]),
    ]
    copies = [
        pltpu.make_async_copy(source, target, sems.at[i]) for i, (source, target) in enumerate(moves)
    ]
    for copy in copies:
        copy.start()
    rows_out[...] = jnp.zeros_like(rows_out)
    for copy in copies[0:6]:
        copy.wait()
    lane = lax.broadcasted_iota(jnp.int32, (4, 128), 1)
    line = lax.broadcasted_iota(jnp.int32, (4, 128), 0)
    inside = lane % 64 - 8 * seat(level)
    codes = jnp.where((inside >= 0) & (inside < 8), EMPTY, 0)
    for reach in range(REACH):
        delta = reach - NEAR
        array_even, from_even = (0, -delta) if -delta in (0, 1) else (1, 2 - delta) if delta > 0 else (2, -delta - 2)
        array_odd, from_odd = (0, 1 - delta) if 1 - delta in (0, 1) else (1, 3 - delta) if delta > 0 else (2, -delta - 1)
        array = jnp.where(odd == 0, array_even, array_odd)
        here = (line == jnp.where((odd_pair == 1) & (array > 0), 3 - array, array)) & (
            lane // 64 == jnp.where(odd == 0, from_even, from_odd)
        )
        for place in range(CAP):
            to = ocean_dst[reach * CAP + place]
            codes = jnp.where(here & (inside == place), jnp.where(to < 32, to, EMPTY), codes)
            to = atmos_dst[reach * CAP + place]
            code = jnp.where(to < 32, 32 + (to % 2) * 16 + to // 2, EMPTY)
            codes = jnp.where(here & (inside == CAP + place), code, codes)
    rows_out[pl.ds(64 * odd + 8 * seat(0) + 4, 4), :] = codes.astype(jnp.float32)
    picks[0:16] = flux[:, 0:128].astype(jnp.float32)
    picks[16:32] = flux[:, 128:256].astype(jnp.float32)
    picks[32:64] = sea[...].astype(jnp.float32)

    def product(row, tile):
        return lax.dot_general(
            row.astype(jnp.bfloat16), tile, (((1,), (1,)), ((), ())), preferred_element_type=jnp.float32
        ).astype(jnp.bfloat16).astype(jnp.float32)

    def chunk(reach):
        def member(target):
            column, lev = PREVIOUS[target + 2] if target < 0 else NEXT[target - 2] if target > 1 else (target, 0)
            return column * 8 + seat(lev)

        return 8 * jnp.where(odd == 0, member(reach - NEAR), member(reach - NEAR + 1))

    copies[8].wait()
    down[8:12] = ocean[pl.ds(0, 64, stride=2), :].reshape(4, 16, 128)
    up[8:12] = ocean[pl.ds(1, 64, stride=2), :].reshape(4, 16, 128)
    copies[6].wait()
    for slot in range(REACH * CAP):
        source = ocean_src[slot]
        row = picks[pl.ds((source % 2) * 16 + source // 2, 1), :]
        rows_out[pl.ds(chunk(slot // CAP) + slot % CAP, 1), :] = product(row, ocean_tiles[slot])
    copies[7].wait()
    for slot in range(REACH * CAP):
        row = picks[pl.ds(32 + atmos_src[slot], 1), :]
        rows_out[pl.ds(chunk(slot // CAP) + CAP + slot % CAP, 1), :] = product(row, atmos_tiles[slot])
    send[...] = rows_out[...].astype(jnp.bfloat16)
    for copy in copies[9:]:
        copy.wait()


def column_kernel(
    atm_mixing, ocean_mixing, atm, ocean, operator, below, above,
    atm_hbm, ocean_hbm, atm_base, ocean_base,
    atm_out, ocean_out, sems,
):
    level = lax.axis_index("lev")
    at_bottom = level == 0
    at_top = level == lax.axis_size("lev") - 1
    for field in range(2):
        low = ocean[pl.ds(64 * field, 32, stride=2), :]
        high = ocean[pl.ds(64 * field + 1, 32, stride=2), :]
        beneath = jnp.where(at_bottom, low, below[8 + 2 * field : 10 + 2 * field].reshape(32, 128))
        overhead = jnp.where(at_top, high, above[8 + 2 * field : 10 + 2 * field].reshape(32, 128))
        ocean_out[pl.ds(64 * field, 32, stride=2), :] = low + ocean_mixing[field : field + 1, 0:1] * (
            high - 2.0 * low + beneath
        )
        ocean_out[pl.ds(64 * field + 1, 32, stride=2), :] = high + ocean_mixing[field : field + 1, 1:2] * (
            overhead - 2.0 * high + low
        )
    ocean_copy = pltpu.make_async_copy(ocean_out, ocean_hbm, sems.at[0])
    ocean_copy.start()
    ocean_base[...] = ocean_out[0:64]
    for field in range(4):
        low, high = atm[field, 0], atm[field, 1]
        beneath = jnp.where(at_bottom, low, jnp.concatenate([below[field], below[4 + field]], axis=1))
        overhead = jnp.where(at_top, high, jnp.concatenate([above[field], above[4 + field]], axis=1))
        mixed_low = low + atm_mixing[0:1, field : field + 1] * (high - 2.0 * low + beneath)
        mixed_high = high + atm_mixing[1:2, field : field + 1] * (overhead - 2.0 * high + low)
        mixed = jnp.concatenate([mixed_low, mixed_high], axis=1)
        lateral = jnp.dot(
            operator[...], mixed, precision=lax.Precision.HIGHEST, preferred_element_type=jnp.float32
        )
        result = mixed + 0.25 * lateral
        atm_out[field, 0] = result[:, 0:256]
        atm_out[field, 1] = result[:, 256:512]
    atm_copy = pltpu.make_async_copy(atm_out, atm_hbm, sems.at[1])
    atm_copy.start()
    atm_base[...] = atm_out[2, 0]
    ocean_copy.wait()
    atm_copy.wait()


def surface_kernel(
    atm_in, ocean_in, atm_base, ocean_base, own, second, first,
    atm_hbm, ocean_hbm,
    atm_rows, ocean_rows, sems,
):
    del atm_in, ocean_in

    @pl.when(lax.axis_index("lev") == 0)
    def _():
        codes = jnp.sum(own[...].astype(jnp.float32).reshape(16, 8, 128), axis=0)
        labels = lax.broadcasted_iota(jnp.int32, (64, 128), 0).astype(jnp.float32)
        total = jnp.zeros((64, 128), jnp.float32)
        for i, inbound in enumerate((own, first, second)):
            onehot = jnp.where(codes[4 + i : 5 + i] == labels, 1.0, 0.0).astype(jnp.bfloat16)
            total = total + jnp.dot(onehot, inbound[...], preferred_element_type=jnp.float32)
        total = 0.5 * total
        ocean_rows[...] = ocean_base[...]
        ocean_rows[pl.ds(0, 32, stride=2), :] = ocean_base[pl.ds(0, 32, stride=2), :] + total[0:32]
        ocean_copy = pltpu.make_async_copy(ocean_rows, ocean_hbm.at[0:64], sems.at[0])
        ocean_copy.start()
        atm_rows[:, 0:128] = atm_base[:, 0:128] + total[32:48]
        atm_rows[:, 128:256] = atm_base[:, 128:256] + total[48:64]
        atm_copy = pltpu.make_async_copy(atm_rows, atm_hbm.at[2, 0], sems.at[1])
        atm_copy.start()
        ocean_copy.wait()
        atm_copy.wait()


def shards(
    atm_state,
    atm_mixing,
    element_operator,
    ocean_state,
    ocean_mixing,
    atm_flux,
    sea_temp,
    ocean_tiles,
    ocean_tile_src,
    ocean_tile_dst,
    atmos_tiles,
    atmos_tile_src,
    atmos_tile_dst,
):
    columns, levels = lax.axis_size("horiz"), lax.axis_size("lev")
    f32, bf16 = jnp.float32, jnp.bfloat16
    vmem = pl.BlockSpec(memory_space=pltpu.VMEM)
    hbm = pl.BlockSpec(memory_space=pltpu.HBM)
    shape = jax.ShapeDtypeStruct
    params = pltpu.CompilerParams(vmem_limit_bytes=8 << 20)
    whole = pltpu.CompilerParams(vmem_limit_bytes=61 << 20)
    ocean_rows = ocean_state.reshape(2, 2, 32, 128).transpose(0, 2, 1, 3).reshape(128, 128)
    send, up, down = pl.pallas_call(
        prep_kernel,
        out_shape=(
            shape((128, 128), bf16),
            shape((12, 16, 128), f32),
            shape((12, 16, 128), f32),
        ),
        in_specs=[hbm] * 10,
        out_specs=(vmem,) * 3,
        scratch_shapes=[pltpu.SMEM((REACH * CAP,), jnp.int32)] * 4
        + [
            pltpu.VMEM((128, 128), f32),
            pltpu.VMEM((16, 256), bf16),
            pltpu.VMEM((32, 128), bf16),
            pltpu.VMEM((REACH * CAP, BLOCK, BLOCK), bf16),
            pltpu.VMEM((REACH * CAP, BLOCK, BLOCK), bf16),
            pltpu.VMEM((64, 128), f32),
            pltpu.VMEM((128, 128), f32),
            pltpu.SemaphoreType.DMA((13,)),
        ],
        compiler_params=whole,
    )(
        ocean_tile_src, ocean_tile_dst, atmos_tile_src, atmos_tile_dst,
        atm_state, ocean_rows, atm_flux, sea_temp.reshape(32, 128), ocean_tiles, atmos_tiles,
    )
    pairs = [[h * levels + 7 - l for h in (g, g + 1) for l in range(levels)] for g in range(0, columns, 2)]
    own = lax.all_to_all(send, ("horiz", "lev"), 0, 0, axis_index_groups=pairs, tiled=True)

    def swap(wave):
        pairs = []
        for g in range(2 - 2 * wave, columns, 4):
            for i in range(2):
                column, lev = NEXT[i]
                pairs.append(((g + column) * levels + lev, (g + 2 + i) % columns * levels))
                column, lev = PREVIOUS[i]
                pairs.append((((g + 2) % columns + column) * levels + lev, (g + i) * levels))
        return lax.ppermute(own, ("horiz", "lev"), pairs)

    second = swap(1)
    first = swap(0)
    below = lax.ppermute(up, "lev", [(i, i + 1) for i in range(levels - 1)])
    above = lax.ppermute(down, "lev", [(i + 1, i) for i in range(levels - 1)])
    atm_next, ocean_next, atm_base, ocean_base = pl.pallas_call(
        column_kernel,
        out_shape=(
            shape(atm_state.shape, f32),
            shape((128, 128), f32),
            shape((16, 256), f32),
            shape((64, 128), f32),
        ),
        in_specs=[vmem] * 7,
        out_specs=(hbm, hbm, vmem, vmem),
        scratch_shapes=[
            pltpu.VMEM(atm_state.shape, f32),
            pltpu.VMEM((128, 128), f32),
            pltpu.SemaphoreType.DMA((2,)),
        ],
        compiler_params=params,
    )(atm_mixing.T, ocean_mixing, atm_state, ocean_rows, element_operator, below, above)
    atm_next, ocean_next = pl.pallas_call(
        surface_kernel,
        out_shape=(shape(atm_state.shape, f32), shape((128, 128), f32)),
        in_specs=[hbm] * 2 + [vmem] * 5,
        out_specs=(hbm, hbm),
        scratch_shapes=[
            pltpu.VMEM((16, 256), f32),
            pltpu.VMEM((64, 128), f32),
            pltpu.SemaphoreType.DMA((2,)),
        ],
        input_output_aliases={0: 0, 1: 1},
        compiler_params=params,
    )(atm_next, ocean_next, atm_base, ocean_base, own, second, first)
    ocean_next = ocean_next.reshape(2, 32, 2, 128).transpose(0, 2, 1, 3).reshape(ocean_state.shape)
    return (atm_next, ocean_next)


def solution(mesh):
    placed = (
        P(None, "lev", None, "horiz"),
        P(None, "lev"),
        P(),
        P(None, "lev", "horiz"),
        P(None, "lev"),
        P(None, "horiz"),
        P("horiz"),
        P(("horiz", "lev"), None, None),
        P(("horiz", "lev")),
        P(("horiz", "lev")),
        P(("horiz", "lev"), None, None),
        P(("horiz", "lev")),
        P(("horiz", "lev")),
    )
    return jax.shard_map(
        shards,
        mesh=mesh,
        in_specs=placed,
        out_specs=(P(None, "lev", None, "horiz"), P(None, "lev", "horiz")),
        check_vma=False,
    )
```

```python
import jax
import jax.numpy as jnp
from jax import lax
from jax.experimental import pallas as pl
from jax.experimental.pallas import tpu as pltpu
from jax.sharding import PartitionSpec as P

BLOCK = 128
NEAR = 2
CAP = 2
REACH = 2 * NEAR + 1
NEXT = ((0, 1), (1, 7))
PREVIOUS = ((1, 6), (1, 2))
EMPTY = 64


def seat(level):
    return 7 - level


def prep_kernel(
    ocean_src_hbm, ocean_dst_hbm, atmos_src_hbm, atmos_dst_hbm,
    atm_hbm, ocean_hbm, flux_hbm, sea_hbm, ocean_tiles_hbm, atmos_tiles_hbm,
    send, up, down,
    ocean_src, ocean_dst, atmos_src, atmos_dst, ocean, flux, sea, ocean_tiles, atmos_tiles, picks, rows_out, sems,
):
    level = lax.axis_index("lev")
    odd = lax.axis_index("horiz") % 2
    odd_pair = lax.axis_index("horiz") // 2 % 2
    moves = [
        (flux_hbm, flux), (sea_hbm, sea), (ocean_src_hbm, ocean_src), (atmos_src_hbm, atmos_src),
        (ocean_dst_hbm, ocean_dst), (atmos_dst_hbm, atmos_dst),
        (ocean_tiles_hbm, ocean_tiles), (atmos_tiles_hbm, atmos_tiles),
        (ocean_hbm, ocean),
        (atm_hbm.at[:, 1, :, 0:128], up.at[0:4]), (atm_hbm.at[:, 1, :, 128:256], up.at[4:8]),
        (atm_hbm.at[:, 0, :, 0:128], down.at[0:4]), (atm_hbm.at[:, 0, :, 128:256], down.at[4:8]),
    ]
    copies = [
        pltpu.make_async_copy(source, target, sems.at[i]) for i, (source, target) in enumerate(moves)
    ]
    for copy in copies:
        copy.start()
    rows_out[...] = jnp.zeros_like(rows_out)
    for copy in copies[0:6]:
        copy.wait()
    lane = lax.broadcasted_iota(jnp.int32, (4, 128), 1)
    line = lax.broadcasted_iota(jnp.int32, (4, 128), 0)
    inside = lane % 64 - 8 * seat(level)
    codes = jnp.where((inside >= 0) & (inside < 8), EMPTY, 0)
    for reach in range(REACH):
        delta = reach - NEAR
        array_even, from_even = (0, -delta) if -delta in (0, 1) else (1, 2 - delta) if delta > 0 else (2, -delta - 2)
        array_odd, from_odd = (0, 1 - delta) if 1 - delta in (0, 1) else (1, 3 - delta) if delta > 0 else (2, -delta - 1)
        array = jnp.where(odd == 0, array_even, array_odd)
        here = (line == jnp.where((odd_pair == 1) & (array > 0), 3 - array, array)) & (
            lane // 64 == jnp.where(odd == 0, from_even, from_odd)
        )
        for place in range(CAP):
            to = ocean_dst[reach * CAP + place]
            codes = jnp.where(here & (inside == place), jnp.where(to < 32, to, EMPTY), codes)
            to = atmos_dst[reach * CAP + place]
            code = jnp.where(to < 32, 32 + (to % 2) * 16 + to // 2, EMPTY)
            codes = jnp.where(here & (inside == CAP + place), code, codes)
    rows_out[pl.ds(64 * odd + 8 * seat(0) + 4, 4), :] = codes.astype(jnp.float32)
    picks[0:16] = flux[:, 0:128].astype(jnp.float32)
    picks[16:32] = flux[:, 128:256].astype(jnp.float32)
    picks[32:64] = sea[...].astype(jnp.float32)

    def product(row, tile):
        return lax.dot_general(
            row.astype(jnp.bfloat16), tile, (((1,), (1,)), ((), ())), preferred_element_type=jnp.float32
        ).astype(jnp.bfloat16).astype(jnp.float32)

    def chunk(reach):
        def member(target):
            column, lev = PREVIOUS[target + 2] if target < 0 else NEXT[target - 2] if target > 1 else (target, 0)
            return column * 8 + seat(lev)

        return 8 * jnp.where(odd == 0, member(reach - NEAR), member(reach - NEAR + 1))

    copies[8].wait()
    down[8:12] = ocean[pl.ds(0, 64, stride=2), :].reshape(4, 16, 128)
    up[8:12] = ocean[pl.ds(1, 64, stride=2), :].reshape(4, 16, 128)
    copies[6].wait()
    for slot in range(REACH * CAP):
        source = ocean_src[slot]
        row = picks[pl.ds((source % 2) * 16 + source // 2, 1), :]
        rows_out[pl.ds(chunk(slot // CAP) + slot % CAP, 1), :] = product(row, ocean_tiles[slot])
    copies[7].wait()
    for slot in range(REACH * CAP):
        row = picks[pl.ds(32 + atmos_src[slot], 1), :]
        rows_out[pl.ds(chunk(slot // CAP) + CAP + slot % CAP, 1), :] = product(row, atmos_tiles[slot])
    send[...] = rows_out[...].astype(jnp.bfloat16)
    for copy in copies[9:]:
        copy.wait()


def column_kernel(
    atm_mixing, ocean_mixing, atm, ocean, operator, below, above,
    atm_hbm, ocean_hbm, atm_base, ocean_base,
    atm_out, ocean_out, sems,
):
    level = lax.axis_index("lev")
    at_bottom = level == 0
    at_top = level == lax.axis_size("lev") - 1
    for field in range(2):
        low = ocean[pl.ds(64 * field, 32, stride=2), :]
        high = ocean[pl.ds(64 * field + 1, 32, stride=2), :]
        beneath = jnp.where(at_bottom, low, below[8 + 2 * field : 10 + 2 * field].reshape(32, 128))
        overhead = jnp.where(at_top, high, above[8 + 2 * field : 10 + 2 * field].reshape(32, 128))
        ocean_out[pl.ds(64 * field, 32, stride=2), :] = low + ocean_mixing[field : field + 1, 0:1] * (
            high - 2.0 * low + beneath
        )
        ocean_out[pl.ds(64 * field + 1, 32, stride=2), :] = high + ocean_mixing[field : field + 1, 1:2] * (
            overhead - 2.0 * high + low
        )
    ocean_copy = pltpu.make_async_copy(ocean_out, ocean_hbm, sems.at[0])
    ocean_copy.start()
    ocean_base[...] = ocean_out[0:64]
    for field in range(4):
        low, high = atm[field, 0], atm[field, 1]
        beneath = jnp.where(at_bottom, low, jnp.concatenate([below[field], below[4 + field]], axis=1))
        overhead = jnp.where(at_top, high, jnp.concatenate([above[field], above[4 + field]], axis=1))
        mixed_low = low + atm_mixing[0:1, field : field + 1] * (high - 2.0 * low + beneath)
        mixed_high = high + atm_mixing[1:2, field : field + 1] * (overhead - 2.0 * high + low)
        mixed = jnp.concatenate([mixed_low, mixed_high], axis=1)
        lateral = jnp.dot(
            operator[...], mixed, precision=lax.Precision.HIGHEST, preferred_element_type=jnp.float32
        )
        result = mixed + 0.25 * lateral
        atm_out[field, 0] = result[:, 0:256]
        atm_out[field, 1] = result[:, 256:512]
    atm_copy = pltpu.make_async_copy(atm_out, atm_hbm, sems.at[1])
    atm_copy.start()
    atm_base[...] = atm_out[2, 0]
    ocean_copy.wait()
    atm_copy.wait()


def surface_kernel(
    atm_in, ocean_in, atm_base, ocean_base, own, second, first,
    atm_hbm, ocean_hbm,
    atm_rows, ocean_rows, sems,
):
    del atm_in, ocean_in

    @pl.when(lax.axis_index("lev") == 0)
    def _():
        codes = jnp.sum(own[...].astype(jnp.float32).reshape(16, 8, 128), axis=0)
        labels = lax.broadcasted_iota(jnp.int32, (64, 128), 0).astype(jnp.float32)
        total = jnp.zeros((64, 128), jnp.float32)
        for i, inbound in enumerate((own, first, second)):
            onehot = jnp.where(codes[4 + i : 5 + i] == labels, 1.0, 0.0).astype(jnp.bfloat16)
            total = total + jnp.dot(onehot, inbound[...], preferred_element_type=jnp.float32)
        total = 0.5 * total
        ocean_rows[...] = ocean_base[...]
        ocean_rows[pl.ds(0, 32, stride=2), :] = ocean_base[pl.ds(0, 32, stride=2), :] + total[0:32]
        ocean_copy = pltpu.make_async_copy(ocean_rows, ocean_hbm.at[0:64], sems.at[0])
        ocean_copy.start()
        atm_rows[:, 0:128] = atm_base[:, 0:128] + total[32:48]
        atm_rows[:, 128:256] = atm_base[:, 128:256] + total[48:64]
        atm_copy = pltpu.make_async_copy(atm_rows, atm_hbm.at[2, 0], sems.at[1])
        atm_copy.start()
        ocean_copy.wait()
        atm_copy.wait()


def shards(
    atm_state,
    atm_mixing,
    element_operator,
    ocean_state,
    ocean_mixing,
    atm_flux,
    sea_temp,
    ocean_tiles,
    ocean_tile_src,
    ocean_tile_dst,
    atmos_tiles,
    atmos_tile_src,
    atmos_tile_dst,
):
    columns, levels = lax.axis_size("horiz"), lax.axis_size("lev")
    f32, bf16 = jnp.float32, jnp.bfloat16
    vmem = pl.BlockSpec(memory_space=pltpu.VMEM)
    hbm = pl.BlockSpec(memory_space=pltpu.HBM)
    shape = jax.ShapeDtypeStruct
    params = pltpu.CompilerParams(vmem_limit_bytes=8 << 20)
    whole = pltpu.CompilerParams(vmem_limit_bytes=61 << 20)
    ocean_rows = ocean_state.reshape(2, 2, 32, 128).transpose(0, 2, 1, 3).reshape(128, 128)
    send, up, down = pl.pallas_call(
        prep_kernel,
        out_shape=(
            shape((128, 128), bf16),
            shape((12, 16, 128), f32),
            shape((12, 16, 128), f32),
        ),
        in_specs=[hbm] * 10,
        out_specs=(vmem,) * 3,
        scratch_shapes=[pltpu.SMEM((REACH * CAP,), jnp.int32)] * 4
        + [
            pltpu.VMEM((128, 128), f32),
            pltpu.VMEM((16, 256), bf16),
            pltpu.VMEM((32, 128), bf16),
            pltpu.VMEM((REACH * CAP, BLOCK, BLOCK), bf16),
            pltpu.VMEM((REACH * CAP, BLOCK, BLOCK), bf16),
            pltpu.VMEM((64, 128), f32),
            pltpu.VMEM((128, 128), f32),
            pltpu.SemaphoreType.DMA((13,)),
        ],
        compiler_params=whole,
    )(
        ocean_tile_src, ocean_tile_dst, atmos_tile_src, atmos_tile_dst,
        atm_state, ocean_rows, atm_flux, sea_temp.reshape(32, 128), ocean_tiles, atmos_tiles,
    )
    pairs = [[h * levels + 7 - l for h in (g, g + 1) for l in range(levels)] for g in range(0, columns, 2)]
    own = lax.all_to_all(send, ("horiz", "lev"), 0, 0, axis_index_groups=pairs, tiled=True)

    def swap(wave):
        pairs = []
        for g in range(2 - 2 * wave, columns, 4):
            for i in range(2):
                column, lev = NEXT[i]
                pairs.append(((g + column) * levels + lev, (g + 2 + i) % columns * levels))
                column, lev = PREVIOUS[i]
                pairs.append((((g + 2) % columns + column) * levels + lev, (g + i) * levels))
        return lax.ppermute(own, ("horiz", "lev"), pairs)

    second = swap(1)
    first = swap(0)
    below = lax.ppermute(up, "lev", [(i, i + 1) for i in range(levels - 1)])
    above = lax.ppermute(down, "lev", [(i + 1, i) for i in range(levels - 1)])
    atm_next, ocean_next, atm_base, ocean_base = pl.pallas_call(
        column_kernel,
        out_shape=(
            shape(atm_state.shape, f32),
            shape((128, 128), f32),
            shape((16, 256), f32),
            shape((64, 128), f32),
        ),
        in_specs=[vmem] * 7,
        out_specs=(hbm, hbm, vmem, vmem),
        scratch_shapes=[
            pltpu.VMEM(atm_state.shape, f32),
            pltpu.VMEM((128, 128), f32),
            pltpu.SemaphoreType.DMA((2,)),
        ],
        compiler_params=params,
    )(atm_mixing.T, ocean_mixing, atm_state, ocean_rows, element_operator, below, above)
    atm_next, ocean_next = pl.pallas_call(
        surface_kernel,
        out_shape=(shape(atm_state.shape, f32), shape((128, 128), f32)),
        in_specs=[hbm] * 2 + [vmem] * 5,
        out_specs=(hbm, hbm),
        scratch_shapes=[
            pltpu.VMEM((16, 256), f32),
            pltpu.VMEM((64, 128), f32),
            pltpu.SemaphoreType.DMA((2,)),
        ],
        input_output_aliases={0: 0, 1: 1},
        compiler_params=params,
    )(atm_next, ocean_next, atm_base, ocean_base, own, second, first)
    ocean_next = ocean_next.reshape(2, 32, 2, 128).transpose(0, 2, 1, 3).reshape(ocean_state.shape)
    return (atm_next, ocean_next)


def solution(mesh):
    placed = (
        P(None, "lev", None, "horiz"),
        P(None, "lev"),
        P(),
        P(None, "lev", "horiz"),
        P(None, "lev"),
        P(None, "horiz"),
        P("horiz"),
        P(("horiz", "lev"), None, None),
        P(("horiz", "lev")),
        P(("horiz", "lev")),
        P(("horiz", "lev"), None, None),
        P(("horiz", "lev")),
        P(("horiz", "lev")),
    )
    return jax.shard_map(
        shards,
        mesh=mesh,
        in_specs=placed,
        out_specs=(P(None, "lev", None, "horiz"), P(None, "lev", "horiz")),
        check_vma=False,
    )
```

```python
import jax
import jax.numpy as jnp
from jax import lax
from jax.experimental import pallas as pl
from jax.experimental.pallas import tpu as pltpu
from jax.sharding import PartitionSpec as P

BLOCK = 128
NEAR = 2
CAP = 2
REACH = 2 * NEAR + 1
NEXT = ((0, 6), (1, 7))
PREVIOUS = ((1, 6), (1, 2))
EMPTY = 64


def seat(level):
    return 7 - level


def prep_kernel(
    ocean_src_hbm, ocean_dst_hbm, atmos_src_hbm, atmos_dst_hbm,
    atm_hbm, ocean_hbm, flux_hbm, sea_hbm, ocean_tiles_hbm, atmos_tiles_hbm,
    send, up, down,
    ocean_src, ocean_dst, atmos_src, atmos_dst, ocean, flux, sea, ocean_tiles, atmos_tiles, picks, rows_out, sems,
):
    level = lax.axis_index("lev")
    odd = lax.axis_index("horiz") % 2
    odd_pair = lax.axis_index("horiz") // 2 % 2
    moves = [
        (flux_hbm, flux), (sea_hbm, sea), (ocean_src_hbm, ocean_src), (atmos_src_hbm, atmos_src),
        (ocean_dst_hbm, ocean_dst), (atmos_dst_hbm, atmos_dst),
        (ocean_tiles_hbm, ocean_tiles), (atmos_tiles_hbm, atmos_tiles),
        (ocean_hbm, ocean),
        (atm_hbm.at[:, 1, :, 0:128], up.at[0:4]), (atm_hbm.at[:, 1, :, 128:256], up.at[4:8]),
        (atm_hbm.at[:, 0, :, 0:128], down.at[0:4]), (atm_hbm.at[:, 0, :, 128:256], down.at[4:8]),
    ]
    copies = [
        pltpu.make_async_copy(source, target, sems.at[i]) for i, (source, target) in enumerate(moves)
    ]
    for copy in copies:
        copy.start()
    rows_out[...] = jnp.zeros_like(rows_out)
    for copy in copies[0:6]:
        copy.wait()
    lane = lax.broadcasted_iota(jnp.int32, (4, 128), 1)
    line = lax.broadcasted_iota(jnp.int32, (4, 128), 0)
    inside = lane % 64 - 8 * seat(level)
    codes = jnp.where((inside >= 0) & (inside < 8), EMPTY, 0)
    for reach in range(REACH):
        delta = reach - NEAR
        array_even, from_even = (0, -delta) if -delta in (0, 1) else (1, 2 - delta) if delta > 0 else (2, -delta - 2)
        array_odd, from_odd = (0, 1 - delta) if 1 - delta in (0, 1) else (1, 3 - delta) if delta > 0 else (2, -delta - 1)
        array = jnp.where(odd == 0, array_even, array_odd)
        here = (line == jnp.where((odd_pair == 1) & (array > 0), 3 - array, array)) & (
            lane // 64 == jnp.where(odd == 0, from_even, from_odd)
        )
        for place in range(CAP):
            to = ocean_dst[reach * CAP + place]
            codes = jnp.where(here & (inside == place), jnp.where(to < 32, to, EMPTY), codes)
            to = atmos_dst[reach * CAP + place]
            code = jnp.where(to < 32, 32 + (to % 2) * 16 + to // 2, EMPTY)
            codes = jnp.where(here & (inside == CAP + place), code, codes)
    rows_out[pl.ds(64 * odd + 8 * seat(0) + 4, 4), :] = codes.astype(jnp.float32)
    picks[0:16] = flux[:, 0:128].astype(jnp.float32)
    picks[16:32] = flux[:, 128:256].astype(jnp.float32)
    picks[32:64] = sea[...].astype(jnp.float32)

    def product(row, tile):
        return lax.dot_general(
            row.astype(jnp.bfloat16), tile, (((1,), (1,)), ((), ())), preferred_element_type=jnp.float32
        ).astype(jnp.bfloat16).astype(jnp.float32)

    def chunk(reach):
        def member(target):
            column, lev = PREVIOUS[target + 2] if target < 0 else NEXT[target - 2] if target > 1 else (target, 0)
            return column * 8 + seat(lev)

        return 8 * jnp.where(odd == 0, member(reach - NEAR), member(reach - NEAR + 1))

    copies[8].wait()
    down[8:12] = ocean[pl.ds(0, 64, stride=2), :].reshape(4, 16, 128)
    up[8:12] = ocean[pl.ds(1, 64, stride=2), :].reshape(4, 16, 128)
    copies[6].wait()
    for slot in range(REACH * CAP):
        source = ocean_src[slot]
        row = picks[pl.ds((source % 2) * 16 + source // 2, 1), :]
        rows_out[pl.ds(chunk(slot // CAP) + slot % CAP, 1), :] = product(row, ocean_tiles[slot])
    copies[7].wait()
    for slot in range(REACH * CAP):
        row = picks[pl.ds(32 + atmos_src[slot], 1), :]
        rows_out[pl.ds(chunk(slot // CAP) + CAP + slot % CAP, 1), :] = product(row, atmos_tiles[slot])
    send[...] = rows_out[...].astype(jnp.bfloat16)
    for copy in copies[9:]:
        copy.wait()


def column_kernel(
    atm_mixing, ocean_mixing, atm, ocean, operator, below, above,
    atm_hbm, ocean_hbm, atm_base, ocean_base,
    atm_out, ocean_out, sems,
):
    level = lax.axis_index("lev")
    at_bottom = level == 0
    at_top = level == lax.axis_size("lev") - 1
    for field in range(2):
        low = ocean[pl.ds(64 * field, 32, stride=2), :]
        high = ocean[pl.ds(64 * field + 1, 32, stride=2), :]
        beneath = jnp.where(at_bottom, low, below[8 + 2 * field : 10 + 2 * field].reshape(32, 128))
        overhead = jnp.where(at_top, high, above[8 + 2 * field : 10 + 2 * field].reshape(32, 128))
        ocean_out[pl.ds(64 * field, 32, stride=2), :] = low + ocean_mixing[field : field + 1, 0:1] * (
            high - 2.0 * low + beneath
        )
        ocean_out[pl.ds(64 * field + 1, 32, stride=2), :] = high + ocean_mixing[field : field + 1, 1:2] * (
            overhead - 2.0 * high + low
        )
    ocean_copy = pltpu.make_async_copy(ocean_out, ocean_hbm, sems.at[0])
    ocean_copy.start()
    ocean_base[...] = ocean_out[0:64]
    for field in range(4):
        low, high = atm[field, 0], atm[field, 1]
        beneath = jnp.where(at_bottom, low, jnp.concatenate([below[field], below[4 + field]], axis=1))
        overhead = jnp.where(at_top, high, jnp.concatenate([above[field], above[4 + field]], axis=1))
        mixed_low = low + atm_mixing[0:1, field : field + 1] * (high - 2.0 * low + beneath)
        mixed_high = high + atm_mixing[1:2, field : field + 1] * (overhead - 2.0 * high + low)
        mixed = jnp.concatenate([mixed_low, mixed_high], axis=1)
        lateral = jnp.dot(
            operator[...], mixed, precision=lax.Precision.HIGHEST, preferred_element_type=jnp.float32
        )
        result = mixed + 0.25 * lateral
        atm_out[field, 0] = result[:, 0:256]
        atm_out[field, 1] = result[:, 256:512]
    atm_copy = pltpu.make_async_copy(atm_out, atm_hbm, sems.at[1])
    atm_copy.start()
    atm_base[...] = atm_out[2, 0]
    ocean_copy.wait()
    atm_copy.wait()


def surface_kernel(
    atm_in, ocean_in, atm_base, ocean_base, own, second, first,
    atm_hbm, ocean_hbm,
    atm_rows, ocean_rows, sems,
):
    del atm_in, ocean_in

    @pl.when(lax.axis_index("lev") == 0)
    def _():
        codes = jnp.sum(own[...].astype(jnp.float32).reshape(16, 8, 128), axis=0)
        labels = lax.broadcasted_iota(jnp.int32, (64, 128), 0).astype(jnp.float32)
        total = jnp.zeros((64, 128), jnp.float32)
        for i, inbound in enumerate((own, first, second)):
            onehot = jnp.where(codes[4 + i : 5 + i] == labels, 1.0, 0.0).astype(jnp.bfloat16)
            total = total + jnp.dot(onehot, inbound[...], preferred_element_type=jnp.float32)
        total = 0.5 * total
        ocean_rows[...] = ocean_base[...]
        ocean_rows[pl.ds(0, 32, stride=2), :] = ocean_base[pl.ds(0, 32, stride=2), :] + total[0:32]
        ocean_copy = pltpu.make_async_copy(ocean_rows, ocean_hbm.at[0:64], sems.at[0])
        ocean_copy.start()
        atm_rows[:, 0:128] = atm_base[:, 0:128] + total[32:48]
        atm_rows[:, 128:256] = atm_base[:, 128:256] + total[48:64]
        atm_copy = pltpu.make_async_copy(atm_rows, atm_hbm.at[2, 0], sems.at[1])
        atm_copy.start()
        ocean_copy.wait()
        atm_copy.wait()


def shards(
    atm_state,
    atm_mixing,
    element_operator,
    ocean_state,
    ocean_mixing,
    atm_flux,
    sea_temp,
    ocean_tiles,
    ocean_tile_src,
    ocean_tile_dst,
    atmos_tiles,
    atmos_tile_src,
    atmos_tile_dst,
):
    columns, levels = lax.axis_size("horiz"), lax.axis_size("lev")
    f32, bf16 = jnp.float32, jnp.bfloat16
    vmem = pl.BlockSpec(memory_space=pltpu.VMEM)
    hbm = pl.BlockSpec(memory_space=pltpu.HBM)
    shape = jax.ShapeDtypeStruct
    params = pltpu.CompilerParams(vmem_limit_bytes=8 << 20)
    whole = pltpu.CompilerParams(vmem_limit_bytes=61 << 20)
    ocean_rows = ocean_state.reshape(2, 2, 32, 128).transpose(0, 2, 1, 3).reshape(128, 128)
    send, up, down = pl.pallas_call(
        prep_kernel,
        out_shape=(
            shape((128, 128), bf16),
            shape((12, 16, 128), f32),
            shape((12, 16, 128), f32),
        ),
        in_specs=[hbm] * 10,
        out_specs=(vmem,) * 3,
        scratch_shapes=[pltpu.SMEM((REACH * CAP,), jnp.int32)] * 4
        + [
            pltpu.VMEM((128, 128), f32),
            pltpu.VMEM((16, 256), bf16),
            pltpu.VMEM((32, 128), bf16),
            pltpu.VMEM((REACH * CAP, BLOCK, BLOCK), bf16),
            pltpu.VMEM((REACH * CAP, BLOCK, BLOCK), bf16),
            pltpu.VMEM((64, 128), f32),
            pltpu.VMEM((128, 128), f32),
            pltpu.SemaphoreType.DMA((13,)),
        ],
        compiler_params=whole,
    )(
        ocean_tile_src, ocean_tile_dst, atmos_tile_src, atmos_tile_dst,
        atm_state, ocean_rows, atm_flux, sea_temp.reshape(32, 128), ocean_tiles, atmos_tiles,
    )
    pairs = [[h * levels + 7 - l for h in (g, g + 1) for l in range(levels)] for g in range(0, columns, 2)]
    own = lax.all_to_all(send, ("horiz", "lev"), 0, 0, axis_index_groups=pairs, tiled=True)

    def swap(wave):
        pairs = []
        for g in range(2 - 2 * wave, columns, 4):
            for i in range(2):
                column, lev = NEXT[i]
                pairs.append(((g + column) * levels + lev, (g + 2 + i) % columns * levels))
                column, lev = PREVIOUS[i]
                pairs.append((((g + 2) % columns + column) * levels + lev, (g + i) * levels))
        return lax.ppermute(own, ("horiz", "lev"), pairs)

    second = swap(1)
    first = swap(0)
    below = lax.ppermute(up, "lev", [(i, i + 1) for i in range(levels - 1)])
    above = lax.ppermute(down, "lev", [(i + 1, i) for i in range(levels - 1)])
    atm_next, ocean_next, atm_base, ocean_base = pl.pallas_call(
        column_kernel,
        out_shape=(
            shape(atm_state.shape, f32),
            shape((128, 128), f32),
            shape((16, 256), f32),
            shape((64, 128), f32),
        ),
        in_specs=[vmem] * 7,
        out_specs=(hbm, hbm, vmem, vmem),
        scratch_shapes=[
            pltpu.VMEM(atm_state.shape, f32),
            pltpu.VMEM((128, 128), f32),
            pltpu.SemaphoreType.DMA((2,)),
        ],
        compiler_params=params,
    )(atm_mixing.T, ocean_mixing, atm_state, ocean_rows, element_operator, below, above)
    atm_next, ocean_next = pl.pallas_call(
        surface_kernel,
        out_shape=(shape(atm_state.shape, f32), shape((128, 128), f32)),
        in_specs=[hbm] * 2 + [vmem] * 5,
        out_specs=(hbm, hbm),
        scratch_shapes=[
            pltpu.VMEM((16, 256), f32),
            pltpu.VMEM((64, 128), f32),
            pltpu.SemaphoreType.DMA((2,)),
        ],
        input_output_aliases={0: 0, 1: 1},
        compiler_params=params,
    )(atm_next, ocean_next, atm_base, ocean_base, own, second, first)
    ocean_next = ocean_next.reshape(2, 32, 2, 128).transpose(0, 2, 1, 3).reshape(ocean_state.shape)
    return (atm_next, ocean_next)


def solution(mesh):
    placed = (
        P(None, "lev", None, "horiz"),
        P(None, "lev"),
        P(),
        P(None, "lev", "horiz"),
        P(None, "lev"),
        P(None, "horiz"),
        P("horiz"),
        P(("horiz", "lev"), None, None),
        P(("horiz", "lev")),
        P(("horiz", "lev")),
        P(("horiz", "lev"), None, None),
        P(("horiz", "lev")),
        P(("horiz", "lev")),
    )
    return jax.shard_map(
        shards,
        mesh=mesh,
        in_specs=placed,
        out_specs=(P(None, "lev", None, "horiz"), P(None, "lev", "horiz")),
        check_vma=False,
    )
```
